256 devices in a mesh: row: 8 (over z_lo, core), col: 32 (over x, z_hi, y).
Axes of the slice: x: 4, y: 4, z: 8 (z_hi: 2, z_lo: 4; z = z_hi * 4 + z_lo), core: 2. Of those that a mesh axis runs over, the one named last changes fastest.
Arguments:
- weights: float32 [16384, 4, 4096], P('row', None, 'col'), may hold values from -6 to 6
- factor: float32 [4, 128, 4, 4096], P(None, 'row', None, 'col'), as said below
- keep_masks: int32 [128, 4, 128], P('row'), may hold values from 0 to 1, as said below
Outputs:
- pruned_weights: float32 [16384, 4, 4096], P('row', None, 'col')
The draws below stay inside these ranges and needn't reach their ends.
Inputs may be any that keep to these rules, and one draw needn't show every extreme that they name: `keep_masks`: 1 keeps a weight; a group's mask of a block keeps exactly 64 of its columns, either two of every four consecutive columns or in no pattern. `factor`: zero where the column comes before the row; the diagonal entries lie between 0.5 and 2.
All inputs are finite; a program needn't handle non-finite values.
Results may differ from the reference program's by a relative error of at most 0.0001.
Values sent between devices are 32-bit elements; how exact they have to be, the bound alone decides.
No kernel may reach another device: no remote copies, remote signals or barrier semaphores. Data moves between devices by JAX's collectives and lax.ppermute only.
A program may use at most 64 MiB of HBM per device.

```python
import jax
import jax.numpy as jnp
from jax import lax

ROWS = 16384
NCOL = 16384
BW = 128
GROUP = 128
NBLK = 4
LOCB = 4
GROUPS = 128
N_COL = 32


def draw_factor(key, part):
    key_off, key_pivot = jax.random.split(key)
    rows_all = NBLK * BW
    row_ids = jnp.arange(rows_all)[:, None]
    column_ids = jnp.arange(NCOL)[None, :]
    off_part = 0.03 * jax.random.normal(key_off, (rows_all, NCOL), jnp.float32)
    pivots = jnp.exp(jax.random.uniform(key_pivot, (rows_all,), jnp.float32, -0.69, 0.69))
    full_rows = jnp.where(column_ids > row_ids, off_part, jnp.where(column_ids == row_ids, pivots[:, None], 0.0))
    return full_rows.astype(jnp.float32).reshape(NBLK, BW, LOCB, BW * N_COL)


def draw_keep_masks(key, part):
    key_mode, key_pick, key_loose = jax.random.split(key, 3)
    patterns = jnp.array([[1, 1, 0, 0], [1, 0, 1, 0], [1, 0, 0, 1], [0, 1, 1, 0], [0, 1, 0, 1], [0, 0, 1, 1]], jnp.int32)
    mode_bits = jax.random.randint(key_mode, (GROUPS, NBLK, 1), 0, 2)
    picked = jax.random.randint(key_pick, (GROUPS, NBLK, BW // 4), 0, 6)
    structured = patterns[picked].reshape(GROUPS, NBLK, BW)
    scores = jax.random.randint(key_loose, (GROUPS, NBLK, BW), 0, 1 << 20) * BW + jnp.arange(BW, dtype=jnp.int32)
    ranks = jnp.argsort(jnp.argsort(scores, axis=-1), axis=-1)
    loose_bits = (ranks < BW // 2).astype(jnp.int32)
    return jnp.where(mode_bits == 1, structured, loose_bits).astype(jnp.int32)


def block_scale(rng, shape, cuts, least, top_value):
    level, own = 1.0, jax.random.fold_in(rng, 6)
    for dim, shards_of in cuts:
        heights = jnp.exp(jax.random.uniform(jax.random.fold_in(own, dim), (shards_of,), jnp.float32, least / len(cuts), top_value / len(cuts)))
        level = level * jnp.repeat(heights, shape[dim] // shards_of).reshape([-1 if axis == dim else 1 for axis in range(len(shape))])
    return level


def centred(own_key, extent, width, limit, cuts=(), held_as=jnp.bfloat16):
    loudness = block_scale(own_key, extent, cuts, -0.22, 0.18) if cuts else 1.0
    values = jax.random.normal(own_key, extent, jnp.float32) * width * loudness
    return jnp.minimum(jnp.maximum(values, -limit), limit).astype(held_as)


def setup_inputs(seed: int = 0) -> dict:
    streams_of = jax.random.split(jax.random.key(seed), 4)
    return {
        "weights": centred(streams_of[0], (ROWS, LOCB, BW * N_COL), 1.0, 6.0, ((0, 8), (2, 32)), jnp.float32),
        "factor": draw_factor(jax.random.fold_in(streams_of[3], 71), 0),
        "keep_masks": draw_keep_masks(jax.random.fold_in(streams_of[3], 71), 0),
    }


def reference(weights, factor, keep_masks):
    matrix = weights.reshape(ROWS, NCOL)
    factor_all = factor.reshape(NBLK * BW, NCOL)
    column_ids = jnp.arange(NCOL)
    position = jnp.arange(BW)
    pruned = jnp.zeros((ROWS, NCOL), jnp.float32)

    def block_step(block, loop_state):
        matrix_now, pruned_now = loop_state
        start = (block * BW).astype(jnp.int32)
        block_slab = lax.dynamic_slice_in_dim(matrix_now, start, BW, 1)
        factor_rows = lax.dynamic_slice_in_dim(factor_all, start, BW, 0)
        triangle = lax.dynamic_slice_in_dim(factor_rows, start, BW, 1)
        keep_block = lax.dynamic_index_in_dim(keep_masks, block, 1, keepdims=False)
        keep_rows = jnp.repeat(keep_block, GROUP, axis=0).astype(jnp.float32)

        def column_step(column, inner_state):
            current, errors, kept = inner_state
            index_now = jnp.asarray(column).astype(jnp.int32)
            column_now = lax.dynamic_index_in_dim(current, index_now, 1, keepdims=False)
            keep_col = lax.dynamic_index_in_dim(keep_rows, index_now, 1, keepdims=False)
            factor_row = lax.dynamic_index_in_dim(triangle, index_now, 0, keepdims=False)
            pivot_value = jnp.sum(jnp.where(position == column, factor_row, 0.0))
            later_row = jnp.where(position > column, factor_row, 0.0)
            kept_col = column_now * keep_col
            error_col = (column_now - kept_col) / pivot_value
            current = current - error_col[:, None] * later_row[None, :]
            errors = lax.dynamic_update_slice_in_dim(errors, error_col[:, None], index_now, 1)
            kept = lax.dynamic_update_slice_in_dim(kept, kept_col[:, None], index_now, 1)
            return current, errors, kept

        empty = jnp.zeros((ROWS, BW), jnp.float32)
        current, errors, kept = lax.fori_loop(0, BW, column_step, (block_slab, empty, empty))
        update = jnp.dot(errors, factor_rows, precision=lax.Precision.HIGHEST, preferred_element_type=jnp.float32)
        after_mask = column_ids >= start + BW
        matrix_now = matrix_now - jnp.where(after_mask[None, :], update, 0.0)
        pruned_now = lax.dynamic_update_slice_in_dim(pruned_now, kept, start, 1)
        return matrix_now, pruned_now

    matrix, pruned = lax.fori_loop(0, NBLK, block_step, (matrix, pruned))
    pruned_cols = column_ids < NBLK * BW
    result = jnp.where(pruned_cols[None, :], pruned, matrix)
    return result.reshape(ROWS, LOCB, BW * N_COL)
```

```python
import functools

import jax
import jax.numpy as jnp
from jax import lax
from jax.experimental import pallas as pl
from jax.experimental.pallas import tpu as pltpu
from jax.sharding import PartitionSpec as P

NX, NZ, NY, NZL = 4, 2, 4, 4
BW = 128
NB = 4
ACT = 64
KACT = NB * ACT
F32, BF16 = jnp.float32, jnp.bfloat16
NN = (((1,), (0,)), ((), ()))
NT = (((1,), (1,)), ((), ()))


def permute(value, move):
    pairs = []
    for row in range(2 * NZL):
        for x in range(NX):
            for z in range(NZ):
                for y in range(NY):
                    target = move(row >> 1, row & 1, x, z, y)
                    if target is not None:
                        zl, core, tx, tz, ty = target
                        pairs.append((device(row >> 1, row & 1, x, z, y), device(zl, core, tx, tz, ty)))
    return lax.ppermute(value, ("row", "col"), pairs)


def device(zl, core, x, z, y):
    return (zl * 2 + core) * (NX * NZ * NY) + (x * NZ + z) * NY + y


def shift(value, dx, dy):
    return permute(value, lambda zl, c, x, z, y: (zl, c, (x + dx) % NX, z, (y + dy) % NY))


def from_first_x(value, dx):
    return permute(value, lambda zl, c, x, z, y: (zl, c, dx, z, y) if x == 0 else None)


def to_second_plane(value):
    return permute(value, lambda zl, c, x, z, y: (zl, c, x, 1, y) if z == 0 else None)


def swap_core(value):
    return permute(value, lambda zl, c, x, z, y: (zl, 1 - c, x, z, y))


def swap_chip(value, j):
    return permute(value, lambda zl, c, x, z, y: (zl ^ j, c, x, z, y))


def owner_chips(value, j, plane):
    return permute(value, lambda zl, c, x, z, y: (zl ^ j, c, 0, plane, y) if x == 0 and z == 0 else None)


def dot(a, b, dims=NN):
    return lax.dot_general(a, b, dims, preferred_element_type=F32)


def split(value):
    high = value.astype(BF16)
    return high, (value - high.astype(F32)).astype(BF16)


def dot3(a, b):
    ah, al = split(a)
    bh, bl = split(b)
    return dot(ah, bh) + (dot(ah, bl) + dot(al, bh))


def compact_kernel(place_ref, w_ref, target_ref, out_ref):
    block = place_ref[0]
    rows = lax.broadcasted_iota(jnp.int32, (ACT, BW), 0) + block * ACT
    for group in range(target_ref.shape[0]):
        pick = (rows == target_ref[group, pl.ds(block, 1), :]).astype(F32).astype(BF16)
        slab = w_ref[pl.ds(group * BW * 4, BW, stride=4), :]
        high, rest = split(slab)
        mid, low = split(slab - high.astype(F32))
        out_ref[group] = dot(pick, high, NT) + (dot(pick, mid, NT) + dot(pick, low, NT))


def solve_kernel(place_ref, *refs):
    mine, others = refs[0:NY], refs[NY : 2 * NY]
    w_ref, target_ref, out_ref, tri_ref, slab_ref = refs[2 * NY :]
    y, group, zl, core = place_ref[0], place_ref[1], place_ref[2], place_ref[3]
    inner = BW // (2 * NZL)
    for s in range(NY):
        block = (y + (NY - s)) & (NY - 1)
        for q, piece in ((0, mine[s]), (1, others[s])):
            for j in range(NZL):
                owner = ((zl ^ j) * 2 + (core ^ q)) * inner
                for b in range(NB):
                    tri_ref[block, pl.ds(pl.multiple_of(b * BW + owner, inner), inner), :] = piece[
                        (j * NB + b) * inner : (j * NB + b + 1) * inner, :
                    ]
        slab_ref[pl.ds(pl.multiple_of(block * ACT, ACT), ACT), :] = w_ref[s]
    rows = lax.broadcasted_iota(jnp.int32, (KACT, BW), 0)
    pick = jnp.concatenate(
        [(rows == target_ref[group, b : b + 1, :]).astype(F32).astype(BF16) for b in range(NB)], axis=1
    )
    full = jnp.concatenate([tri_ref[b] for b in range(NB)], axis=1)
    high, low = split(full)
    high = dot(pick, high).astype(BF16)
    low = dot(pick, low).astype(BF16)
    active = dot(high, pick, NT) + dot(low, pick, NT)
    row_id = lax.broadcasted_iota(jnp.int32, (KACT, KACT), 0)
    col_ids = lax.broadcasted_iota(jnp.int32, (KACT, KACT), 1)
    diagonal = jnp.where(row_id == col_ids, active, 0.0)
    scale_down = 1.0 / jnp.sum(diagonal, axis=1, keepdims=True)
    scale_across = 1.0 / jnp.sum(diagonal, axis=0, keepdims=True)
    strict = jnp.where(row_id < col_ids, active, 0.0) * scale_down
    differ = row_id ^ col_ids
    inverse = jnp.where(row_id == col_ids, 1.0, 0.0) - jnp.where(differ == 1, strict, 0.0)
    size = 2
    while size < KACT:
        cross = jnp.where((differ >= size) & (differ < 2 * size), strict, 0.0)
        inverse = inverse - dot3(inverse, dot3(cross, inverse))
        size *= 2
    slab = slab_ref[...].T
    out_ref[...] = dot3(slab, inverse) * scale_across


def layout_kernel(place_ref, *refs):
    mine, others = refs[0:NZL], refs[NZL]
    high_ref, low_ref = refs[NZL + 1 :]
    zl, core = place_ref[0], place_ref[1]
    inner = BW // (2 * NZL)
    for j in range(NZL):
        for q in range(2):
            owner = ((zl ^ j) * 2 + (core ^ q)) * inner
            for b in range(NB):
                for l in range(4):
                    rows = pl.ds(b * inner * 4 + l, inner, stride=4)
                    value = mine[j][rows, :] if q == 0 else others[j, rows, :]
                    high, low = split(value)
                    here = (pl.ds(pl.multiple_of(b * BW + owner, inner), inner), slice(l * BW, (l + 1) * BW))
                    high_ref[here] = high
                    low_ref[here] = low


def update_kernel(place_ref, groups_ref, w_ref, high_ref, low_ref, target_ref, *refs, pieces, first):
    errors = refs[: len(pieces[0])]
    refs = refs[len(pieces[0]) :]
    out_ref, buf_ref, pick_ref, ed_high, ed_low, upd_ref, in_sem, out_sem = refs[0 if first else 1 :]
    y, owner = place_ref[0], place_ref[1]
    half = BW // 2
    plan = pieces[1]
    size = 4 * BW

    def rows_of(k):
        return pl.ds(pl.multiple_of(groups_ref[k] * size, size), size)

    count = len(plan)
    for k in range(count):
        pltpu.make_async_copy(w_ref.at[rows_of(k)], buf_ref.at[k], in_sem.at[k]).start()
    pick_ref[...] = jnp.zeros_like(pick_ref)
    rows = lax.broadcasted_iota(jnp.int32, (ACT, BW), 0)
    start = 0
    while start < count:
        many = min(3, count - start)
        for k in range(start, start + many):
            group = groups_ref[k]
            for b in range(NB):
                pick = (rows + b * ACT == target_ref[group, b : b + 1, :]).astype(F32).astype(BF16)
                pick_ref[b * ACT : (b + 1) * ACT, b * BW : (b + 1) * BW] = pick
            pick = pick_ref[...]
            here = slice((k - start) * BW, (k - start + 1) * BW)
            what = plan[k]
            if len(what) == 1:
                value = errors[what[0]][...]
            else:
                (r0, i0), (r1, i1) = what
                value = jnp.concatenate([errors[r0][i0], errors[r1][i1]], axis=0)
            high, low = split(value)
            ed_high[here, :] = dot(high, pick).astype(BF16)
            ed_low[here, :] = dot(low, pick).astype(BF16)
        span = slice(0, many * BW)
        upd_ref[span, :] = dot(ed_high[span, :], high_ref[...]) + (
            dot(ed_high[span, :], low_ref[...]) + dot(ed_low[span, :], high_ref[...])
        )
        for k in range(start, start + many):
            group = groups_ref[k]
            pltpu.make_async_copy(w_ref.at[rows_of(k)], buf_ref.at[k], in_sem.at[k]).wait()
            kept = (target_ref[group, pl.ds(y, 1), :] < 0) | (owner == 0)
            for l in range(4):
                here = pl.ds(l, BW, stride=4)
                value = buf_ref[k, here, :] - upd_ref[(k - start) * BW : (k - start + 1) * BW, l * BW : (l + 1) * BW]
                if l == 0:
                    value = jnp.where(kept, value, 0.0)
                buf_ref[k, here, :] = value
            pltpu.make_async_copy(buf_ref.at[k], out_ref.at[rows_of(k)], out_sem.at[k]).start()
        start += many
    for k in range(count):
        pltpu.make_async_copy(buf_ref.at[k], out_ref.at[rows_of(k)], out_sem.at[k]).wait()


def whole(shape):
    return pl.BlockSpec(shape, lambda *_: (0,) * len(shape))


SMEM = pl.BlockSpec(memory_space=pltpu.SMEM)


ANY = pl.BlockSpec(memory_space=pl.ANY)


def scalars(*values):
    return jnp.stack(values).astype(jnp.int32)


def update(place, groups, flat, high, low, target, errors, plan, earlier=None):
    count = len(plan)
    first = earlier is None
    operands = [place, groups, flat, high, low, target, *errors] + ([] if first else [earlier])
    specs = [SMEM, SMEM, ANY] + [whole(v.shape) for v in operands[3 : 6 + len(errors)]] + ([] if first else [ANY])
    return pl.pallas_call(
        functools.partial(update_kernel, pieces=(errors, plan), first=first),
        out_shape=jax.ShapeDtypeStruct(flat.shape, F32),
        in_specs=specs,
        out_specs=ANY,
        input_output_aliases={} if first else {len(operands) - 1: 0},
        scratch_shapes=[
            pltpu.VMEM((count, 4 * BW, BW), F32),
            pltpu.VMEM((KACT, NB * BW), BF16),
            pltpu.VMEM((3 * BW, NB * BW), BF16),
            pltpu.VMEM((3 * BW, NB * BW), BF16),
            pltpu.VMEM((3 * BW, 4 * BW), F32),
            pltpu.SemaphoreType.DMA((count,)),
            pltpu.SemaphoreType.DMA((count,)),
        ],
        compiler_params=pltpu.CompilerParams(vmem_limit_bytes=40 << 20),
        cost_estimate=pl.CostEstimate(flops=count * 2**28, bytes_accessed=count * 2**19, transcendentals=0),
    )(*operands)


def local(weights, factor, keep_masks):
    me, row = lax.axis_index("col"), lax.axis_index("row")
    x, z, y = me >> 3, (me >> 2) & 1, me & 3
    zl, core = row >> 1, row & 1
    groups = keep_masks.shape[0]
    rows = weights.shape[0]
    flat = weights.reshape(rows * 4, BW)
    barrier = lax.optimization_barrier

    with jax.named_scope("triangle_rows"):
        mine = factor[:, :, 0, :].reshape(-1, BW)
        near = [owner_chips(mine, j, 0) for j in range(1, NZL)]
        far = [owner_chips(mine, j, 1) for j in range(NZL)]

    with jax.named_scope("compact"):
        pruned = 1 - keep_masks
        before = jnp.triu(jnp.ones((BW, BW), BF16), 1)
        rank = lax.dot_general(
            pruned.astype(BF16), before, (((2,), (0,)), ((), ())), preferred_element_type=F32
        ).astype(jnp.int32)
        target = jnp.where(pruned == 1, rank + ACT * jnp.arange(NB, dtype=jnp.int32)[None, :, None], -1)
        compact = pl.pallas_call(
            compact_kernel,
            out_shape=jax.ShapeDtypeStruct((groups, ACT, BW), F32),
            in_specs=[SMEM, whole(flat.shape), whole((groups, NB, BW))],
            out_specs=whole((groups, ACT, BW)),
            grid=(1,),
            compiler_params=pltpu.CompilerParams(vmem_limit_bytes=40 << 20),
            cost_estimate=pl.CostEstimate(flops=2**30, bytes_accessed=2**24, transcendentals=0),
        )(scalars(y), flat, target)

    with jax.named_scope("triangle_x"):
        tri = jnp.stack(
            [jnp.where(z == 1, far[0], mine)] + [near[j - 1] + far[j] for j in range(1, NZL)]
        ).reshape(-1, BW)
        tri, compact = barrier((tri, compact))
        moved = [from_first_x(tri, dx) for dx in (1, 2, 3)]

    with jax.named_scope("slab_y"):
        pieces = [lax.dynamic_slice_in_dim(compact, y * NX, NX, 0)]
        for s in (1, 2, 3):
            piece = lax.dynamic_slice_in_dim(compact, ((y + s) & 3) * NX, NX, 0)
            pieces.append(shift(piece, 0, s))

    with jax.named_scope("factor_chips"):
        tri, moved, factor = barrier((tri, moved, factor))
        here = factor.reshape(-1, BW)
        chips = [here] + [swap_chip(here, j) for j in range(1, NZL)]

    with jax.named_scope("triangle_y"):
        tri = jnp.where(x == 0, tri, moved[0] + moved[1] + moved[2])
        tris = [tri] + [shift(tri, 0, s) for s in (1, 2, 3)]

    with jax.named_scope("slab_x"):
        stacked = jnp.stack(pieces, axis=1)
        moved = [from_first_x(stacked[dx], dx) for dx in (1, 2, 3)]
        slab = jnp.where(x == 0, stacked[0], moved[0] + moved[1] + moved[2])

    with jax.named_scope("slab_z"):
        slab = jnp.where(z == 1, to_second_plane(slab), slab)

    with jax.named_scope("triangle_core"):
        others = [swap_core(piece) for piece in tris]

    with jax.named_scope("factor_core"):
        other_chips = swap_core(jnp.stack(chips))

    with jax.named_scope("solve"):
        errors = pl.pallas_call(
            solve_kernel,
            out_shape=jax.ShapeDtypeStruct((BW, KACT), F32),
            in_specs=[SMEM] + [whole((NB * BW // 2, BW))] * 8 + [whole((NB, ACT, BW)), whole((groups, NB, BW))],
            out_specs=whole((BW, KACT)),
            grid=(1,),
            scratch_shapes=[pltpu.VMEM((NB, NB * BW, BW), F32), pltpu.VMEM((KACT, BW), F32)],
            compiler_params=pltpu.CompilerParams(vmem_limit_bytes=32 << 20),
            cost_estimate=pl.CostEstimate(flops=2**31, bytes_accessed=2**21, transcendentals=0),
        )(scalars(y, y * NX + x, zl, core), *tris, *others, slab, target)

    with jax.named_scope("layout"):
        high, low = pl.pallas_call(
            layout_kernel,
            out_shape=[jax.ShapeDtypeStruct((NB * BW, 4 * BW), BF16)] * 2,
            in_specs=[SMEM] + [whole((4 * BW // 2, BW))] * 4 + [whole((4, 4 * BW // 2, BW))],
            out_specs=[whole((NB * BW, 4 * BW))] * 2,
            grid=(1,),
            cost_estimate=pl.CostEstimate(flops=2**20, bytes_accessed=2**22, transcendentals=0),
        )(scalars(zl, core), *chips, other_chips)

    with jax.named_scope("errors_near"):
        half = BW // 2
        by_y = [shift(errors, 0, s) for s in (1, 2, 3)]
        by_x = [shift(errors, t, 0) for t in (1, 2, 3)]
        by_x, by_y, high, low = barrier((by_x, by_y, high, low))

    with jax.named_scope("errors_far"):
        top = jnp.stack([piece[:half] for piece in by_y])
        bottom = jnp.stack([piece[half:] for piece in by_x])
        top_x = [shift(top, t, 0) for t in (1, 2, 3)]
        bottom_y = [shift(bottom, 0, s) for s in (1, 2, 3)]

    with jax.named_scope("update"):
        place = scalars(y, ((x == 0) & (z == 0)).astype(jnp.int32))

        def group_of(s, t):
            return ((y + (NY - s)) & 3) * NX + ((x + (NX - t)) & 3)

        first = [(0, 0)] + [(s, 0) for s in (1, 2, 3)] + [(0, t) for t in (1, 2, 3)]
        out = update(
            place, scalars(*[group_of(*p) for p in first]), flat, high, low, target,
            [errors, *by_y, *by_x], [(k,) for k in range(7)],
        )
        out, top_x, bottom_y = barrier((out, top_x, bottom_y))
        second = [(s, t) for s in (1, 2, 3) for t in (1, 2, 3)]
        out = update(
            place, scalars(*[group_of(*p) for p in second]), flat, high, low, target,
            [*top_x, *bottom_y], [((t - 1, s - 1), (3 + s - 1, t - 1)) for s, t in second], out,
        )
    return out.reshape(weights.shape)


def solution(mesh):
    placed = (P("row", None, "col"), P(None, "row", None, "col"), P("row", None, None))
    return jax.shard_map(
        local, mesh=mesh, in_specs=placed, out_specs=P("row", None, "col"), check_vma=False
    )
```

```python
import functools

import jax
import jax.numpy as jnp
from jax import lax
from jax.experimental import pallas as pl
from jax.experimental.pallas import tpu as pltpu
from jax.sharding import PartitionSpec as P

NX, NZ, NY, NZL = 4, 2, 4, 4
BW = 128
NB = 4
ACT = 64
KACT = NB * ACT
F32, BF16 = jnp.float32, jnp.bfloat16
NN = (((1,), (0,)), ((), ()))
NT = (((1,), (1,)), ((), ()))


def permute(value, move):
    pairs = []
    for row in range(2 * NZL):
        for x in range(NX):
            for z in range(NZ):
                for y in range(NY):
                    target = move(row >> 1, row & 1, x, z, y)
                    if target is not None:
                        zl, core, tx, tz, ty = target
                        pairs.append((device(row >> 1, row & 1, x, z, y), device(zl, core, tx, tz, ty)))
    return lax.ppermute(value, ("row", "col"), pairs)


def device(zl, core, x, z, y):
    return (zl * 2 + core) * (NX * NZ * NY) + (x * NZ + z) * NY + y


def shift(value, dx, dy, planes=(0, 1)):
    return permute(
        value, lambda zl, c, x, z, y: (zl, c, (x + dx) % NX, z, (y + dy) % NY) if z in planes else None
    )


def from_first_x(value, dx):
    return permute(value, lambda zl, c, x, z, y: (zl, c, dx, z, y) if x == 0 and z == 0 else None)


def to_second_plane(value):
    return permute(value, lambda zl, c, x, z, y: (zl, c, x, 1, y) if z == 0 else None)


def swap_core(value, planes=(0, 1)):
    return permute(value, lambda zl, c, x, z, y: (zl, 1 - c, x, z, y) if z in planes else None)


def swap_chip(value, j, owners=False):
    return permute(
        value,
        lambda zl, c, x, z, y: (zl ^ j, c, x, z, y) if not owners or (x == 0 and z == 0) else None,
    )


def dot(a, b, dims=NN):
    return lax.dot_general(a, b, dims, preferred_element_type=F32)


def split(value):
    high = value.astype(BF16)
    return high, (value - high.astype(F32)).astype(BF16)


def dot3(a, b):
    ah, al = split(a)
    bh, bl = split(b)
    return dot(jnp.concatenate([ah, ah, al], axis=1), jnp.concatenate([bh, bl, bh], axis=0))


def compact_kernel(place_ref, w_ref, target_ref, out_ref):
    block = place_ref[1]
    rows = lax.broadcasted_iota(jnp.int32, (ACT, BW), 0) + block * ACT
    for group in range(target_ref.shape[0]):
        pick = (rows == target_ref[group, pl.ds(block, 1), :]).astype(F32).astype(BF16)
        slab = w_ref[pl.ds(group * BW * 4, BW, stride=4), :]
        high, rest = split(slab)
        mid, low = split(slab - high.astype(F32))
        out_ref[group] = dot(pick, high, NT) + (dot(pick, mid, NT) + dot(pick, low, NT))


def solve_kernel(place_ref, *refs):
    mine, others, far = refs[0:NY], refs[NY], refs[NY + 1]
    w_ref, target_ref, out_ref, tri_ref, slab_ref = refs[NY + 2 :]
    x, y, zl, core = place_ref[0], place_ref[1], place_ref[2], place_ref[3]
    group = y * NX + x
    inner = BW // (2 * NZL)
    for s in range(NY):
        block = (y + (NY - s)) & (NY - 1)
        for q, piece in ((0, mine[s]), (1, others if s == 0 else far.at[s - 1])):
            for j in range(NZL):
                owner = ((zl ^ j) * 2 + (core ^ q)) * inner
                for b in range(NB):
                    tri_ref[block, pl.ds(pl.multiple_of(b * BW + owner, inner), inner), :] = piece[
                        (j * NB + b) * inner : (j * NB + b + 1) * inner, :
                    ]
        slab_ref[pl.ds(pl.multiple_of(block * ACT, ACT), ACT), :] = (
            w_ref[...] if s == 0 else mine[s][NB * BW // 2 :, :]
        )
    rows = lax.broadcasted_iota(jnp.int32, (KACT, BW), 0)
    pick = jnp.concatenate(
        [(rows == target_ref[group, b : b + 1, :]).astype(F32).astype(BF16) for b in range(NB)], axis=1
    )
    full = jnp.concatenate([tri_ref[b] for b in range(NB)], axis=1)
    high, low = split(full)
    high = dot(pick, high).astype(BF16)
    low = dot(pick, low).astype(BF16)
    active = dot(high, pick, NT) + dot(low, pick, NT)
    row_id = lax.broadcasted_iota(jnp.int32, (KACT, KACT), 0)
    col_ids = lax.broadcasted_iota(jnp.int32, (KACT, KACT), 1)
    diagonal = jnp.where(row_id == col_ids, active, 0.0)
    scale_down = 1.0 / jnp.sum(diagonal, axis=1, keepdims=True)
    scale_across = 1.0 / jnp.sum(diagonal, axis=0, keepdims=True)
    strict = jnp.where(row_id < col_ids, active, 0.0) * scale_down
    differ = row_id ^ col_ids
    inverse = jnp.where(row_id == col_ids, 1.0, 0.0) - jnp.where(differ == 1, strict, 0.0)
    size = 2
    while size < KACT:
        cross = jnp.where((differ >= size) & (differ < 2 * size), strict, 0.0)
        inverse = inverse - dot3(inverse, dot3(cross, inverse))
        size *= 2
    slab = slab_ref[...].T
    out_ref[...] = dot3(slab, inverse) * scale_across


def layout_kernel(place_ref, *refs):
    mine, others = refs[0:2], refs[2:4]
    out_ref = refs[4]
    zl, core = place_ref[2], place_ref[3]
    inner = BW // (2 * NZL)
    for j in range(NZL):
        for q in range(2):
            owner = ((zl ^ j) * 2 + (core ^ q)) * inner
            for b in range(NB):
                for l in range(4):
                    rows = pl.ds(b * inner * 4 + l, inner, stride=4)
                    value = (mine, others)[q][j // 2][j % 2, rows, :]
                    high, low = split(value)
                    for part, piece in enumerate((high, low, high)):
                        start = pl.multiple_of((part * NB + b) * BW + owner, inner)
                        out_ref[pl.ds(start, inner), l * BW : (l + 1) * BW] = piece


def update_kernel(place_ref, w_ref, spread_ref, target_ref, *refs, pieces, first):
    errors = refs[: len(pieces[0])]
    refs = refs[len(pieces[0]) :]
    out_ref, buf_ref, pick_ref, ed_ref, upd_ref, in_sem, out_sem = refs[0 if first else 1 :]
    x, y, owner = place_ref[0], place_ref[1], place_ref[4]
    plan, places = pieces[1], pieces[2]
    which = [((y + (NY - s)) & 3) * NX + ((x + (NX - t)) & 3) for s, t in places]
    size = 4 * BW

    def rows_of(k):
        return pl.ds(pl.multiple_of(which[k] * size, size), size)

    count = len(plan)
    for k in range(count):
        pltpu.make_async_copy(w_ref.at[rows_of(k)], buf_ref.at[k], in_sem.at[k]).start()
    pick_ref[...] = jnp.zeros_like(pick_ref)
    rows = lax.broadcasted_iota(jnp.int32, (ACT, BW), 0)
    start = 0
    while start < count:
        many = min(3, count - start)
        for k in range(start, start + many):
            group = which[k]
            for b in range(NB):
                pick = (rows + b * ACT == target_ref[group, b : b + 1, :]).astype(F32).astype(BF16)
                pick_ref[b * ACT : (b + 1) * ACT, b * BW : (b + 1) * BW] = pick
            pick = pick_ref[...]
            here = slice((k - start) * BW, (k - start + 1) * BW)
            what = plan[k]
            if len(what) == 1:
                value = errors[what[0]][...]
            else:
                (r0, i0), (r1, i1) = what
                value = jnp.concatenate([errors[r0][i0], errors[r1][i1]], axis=0)
            high, low = split(value)
            wide = NB * BW
            high = dot(high, pick).astype(BF16)
            ed_ref[here, 0:wide] = high
            ed_ref[here, wide : 2 * wide] = high
            ed_ref[here, 2 * wide :] = dot(low, pick).astype(BF16)
        span = slice(0, many * BW)
        upd_ref[span, :] = dot(ed_ref[span, :], spread_ref[...])
        for k in range(start, start + many):
            group = which[k]
            pltpu.make_async_copy(w_ref.at[rows_of(k)], buf_ref.at[k], in_sem.at[k]).wait()
            kept = (target_ref[group, pl.ds(y, 1), :] < 0) | (owner == 0)
            for l in range(4):
                here = pl.ds(l, BW, stride=4)
                value = buf_ref[k, here, :] - upd_ref[(k - start) * BW : (k - start + 1) * BW, l * BW : (l + 1) * BW]
                if l == 0:
                    value = jnp.where(kept, value, 0.0)
                buf_ref[k, here, :] = value
            pltpu.make_async_copy(buf_ref.at[k], out_ref.at[rows_of(k)], out_sem.at[k]).start()
        start += many
    for k in range(count):
        pltpu.make_async_copy(buf_ref.at[k], out_ref.at[rows_of(k)], out_sem.at[k]).wait()


def whole(shape):
    return pl.BlockSpec(shape, lambda *_: (0,) * len(shape))


SMEM = pl.BlockSpec(memory_space=pltpu.SMEM)


ANY = pl.BlockSpec(memory_space=pl.ANY)


def scalars(*values):
    return jnp.stack([jnp.asarray(v, jnp.int32) for v in values])


def update(place, flat, spread, target, errors, plan, places, earlier=None):
    count = len(plan)
    first = earlier is None
    operands = [place, flat, spread, target, *errors] + ([] if first else [earlier])
    specs = [SMEM, ANY] + [whole(v.shape) for v in operands[2 : 4 + len(errors)]] + ([] if first else [ANY])
    return pl.pallas_call(
        functools.partial(update_kernel, pieces=(errors, plan, places), first=first),
        out_shape=jax.ShapeDtypeStruct(flat.shape, F32),
        in_specs=specs,
        out_specs=ANY,
        input_output_aliases={} if first else {len(operands) - 1: 0},
        scratch_shapes=[
            pltpu.VMEM((count, 4 * BW, BW), F32),
            pltpu.VMEM((KACT, NB * BW), BF16),
            pltpu.VMEM((3 * BW, 3 * NB * BW), BF16),
            pltpu.VMEM((3 * BW, 4 * BW), F32),
            pltpu.SemaphoreType.DMA((count,)),
            pltpu.SemaphoreType.DMA((count,)),
        ],
        compiler_params=pltpu.CompilerParams(vmem_limit_bytes=50 << 20),
        cost_estimate=pl.CostEstimate(flops=count * 2**28, bytes_accessed=count * 2**19, transcendentals=0),
    )(*operands)


def local(weights, factor, keep_masks):
    me, row = lax.axis_index("col"), lax.axis_index("row")
    x, z, y = me >> 3, (me >> 2) & 1, me & 3
    zl, core = row >> 1, row & 1
    groups = keep_masks.shape[0]
    rows = weights.shape[0]
    flat = weights.reshape(rows * 4, BW)
    barrier = lax.optimization_barrier
    place = scalars(x, y, zl, core, (x == 0) & (z == 0))

    with jax.named_scope("triangle_rows"):
        here = factor.reshape(-1, BW)
        near = swap_chip(here, 1)

    with jax.named_scope("compact"):
        pruned = 1 - keep_masks
        before = jnp.triu(jnp.ones((BW, BW), BF16), 1)
        rank = lax.dot_general(
            pruned.astype(BF16), before, (((2,), (0,)), ((), ())), preferred_element_type=F32
        ).astype(jnp.int32)
        target = jnp.where(pruned == 1, rank + ACT * jnp.arange(NB, dtype=jnp.int32)[None, :, None], -1)
        compact = pl.pallas_call(
            compact_kernel,
            out_shape=jax.ShapeDtypeStruct((groups, ACT, BW), F32),
            in_specs=[SMEM, whole(flat.shape), whole((groups, NB, BW))],
            out_specs=whole((groups, ACT, BW)),
            grid=(1,),
            compiler_params=pltpu.CompilerParams(vmem_limit_bytes=40 << 20),
            cost_estimate=pl.CostEstimate(flops=2**30, bytes_accessed=2**24, transcendentals=0),
        )(place, flat, target)

    with jax.named_scope("triangle_pairs"):
        near, compact = barrier((near, compact))
        chips = [jnp.stack([here, near])]
        pair = chips[0].reshape(2, -1, 4, BW)[:, :, 0, :]
        pair_far = swap_chip(pair, 2, True)

    with jax.named_scope("slab_x"):
        by_owner = compact.reshape(NY, NX, ACT, BW)
        moved = [from_first_x(by_owner[:, dx], dx) for dx in (1, 2, 3)]
        slabs = jnp.where(x == 0, by_owner[:, 0], moved[0] + moved[1] + moved[2])

    with jax.named_scope("triangle_x"):
        tri = jnp.concatenate([pair, pair_far]).reshape(-1, BW)
        tri, chips = barrier((tri, chips))
        moved = [from_first_x(tri, dx) for dx in (1, 2, 3)]

    with jax.named_scope("factor_chips"):
        chips = [chips[0], swap_chip(chips[0], 2)]

    with jax.named_scope("triangle_y"):
        tri = jnp.where(x == 0, tri, moved[0] + moved[1] + moved[2])
        mixed = []
        for s in (1, 2, 3):
            piece = lax.dynamic_index_in_dim(slabs, (y + s) & 3, 0, keepdims=False)
            mixed.append(shift(jnp.concatenate([tri, piece]), 0, s, (0,)))
        slab = lax.dynamic_index_in_dim(slabs, y, 0, keepdims=False)

    with jax.named_scope("triangle_core"):
        tri, mixed, chips = barrier((tri, mixed, chips))
        others = swap_core(jnp.stack([piece[: NB * BW // 2] for piece in mixed]), (0,))
        other = swap_core(tri, (0,))

    with jax.named_scope("factor_core"):
        other_chips = [swap_core(piece) for piece in chips]

    with jax.named_scope("solve"):
        errors = pl.pallas_call(
            solve_kernel,
            out_shape=jax.ShapeDtypeStruct((BW, KACT), F32),
            in_specs=[SMEM, whole(tri.shape)] + [whole(mixed[0].shape)] * 3
            + [whole(v.shape) for v in (other, others, slab, target)],
            out_specs=whole((BW, KACT)),
            grid=(1,),
            scratch_shapes=[pltpu.VMEM((NB, NB * BW, BW), F32), pltpu.VMEM((KACT, BW), F32)],
            compiler_params=pltpu.CompilerParams(vmem_limit_bytes=32 << 20),
            cost_estimate=pl.CostEstimate(flops=2**31, bytes_accessed=2**21, transcendentals=0),
        )(place, tri, *mixed, other, others, slab, target)

    with jax.named_scope("errors_plane"):
        errors, other_chips = barrier((errors, other_chips))
        errors = jnp.where(z == 1, to_second_plane(errors), errors)

    with jax.named_scope("errors_near"):
        half = BW // 2
        by_y = [shift(errors, 0, s) for s in (1, 2, 3)]
        by_x = [shift(errors, t, 0) for t in (1, 2, 3)]

    with jax.named_scope("layout"):
        spread = pl.pallas_call(
            layout_kernel,
            out_shape=jax.ShapeDtypeStruct((3 * NB * BW, 4 * BW), BF16),
            in_specs=[SMEM] + [whole((2, 4 * BW // 2, BW))] * 4,
            out_specs=whole((3 * NB * BW, 4 * BW)),
            grid=(1,),
            compiler_params=pltpu.CompilerParams(vmem_limit_bytes=16 << 20),
            cost_estimate=pl.CostEstimate(flops=2**28, bytes_accessed=2**23, transcendentals=0),
        )(place, *chips, *other_chips)

    with jax.named_scope("errors_far"):
        top = jnp.stack([piece[:half] for piece in by_y])
        bottom = jnp.stack([piece[half:] for piece in by_x])
        top_x = [shift(top, t, 0) for t in (1, 2, 3)]
        bottom_y = [shift(bottom, 0, s) for s in (1, 2, 3)]

    with jax.named_scope("update"):
        first = [(0, 0)] + [(s, 0) for s in (1, 2, 3)] + [(0, t) for t in (1, 2, 3)]
        out = update(
            place, flat, spread, target,
            [errors, *by_y, *by_x], [(k,) for k in range(7)], first,
        )
        out, top_x, bottom_y = barrier((out, top_x, bottom_y))
        second = [(s, t) for s in (1, 2, 3) for t in (1, 2, 3)]
        out = update(
            place, flat, spread, target,
            [*top_x, *bottom_y], [((t - 1, s - 1), (3 + s - 1, t - 1)) for s, t in second], second, out,
        )
    return out.reshape(weights.shape)


def solution(mesh):
    placed = (P("row", None, "col"), P(None, "row", None, "col"), P("row", None, None))
    return jax.shard_map(
        local, mesh=mesh, in_specs=placed, out_specs=P("row", None, "col"), check_vma=False
    )
```

```python
import functools

import jax
import jax.numpy as jnp
from jax import lax
from jax.experimental import pallas as pl
from jax.experimental.pallas import tpu as pltpu
from jax.sharding import PartitionSpec as P

NX, NZ, NY, NZL = 4, 2, 4, 4
BW = 128
NB = 4
ACT = 64
KACT = NB * ACT
F32, BF16 = jnp.float32, jnp.bfloat16
NN = (((1,), (0,)), ((), ()))
NT = (((1,), (1,)), ((), ()))


def permute(value, move):
    pairs = []
    for row in range(2 * NZL):
        for x in range(NX):
            for z in range(NZ):
                for y in range(NY):
                    target = move(row >> 1, row & 1, x, z, y)
                    if target is not None:
                        zl, core, tx, tz, ty = target
                        pairs.append((device(row >> 1, row & 1, x, z, y), device(zl, core, tx, tz, ty)))
    return lax.ppermute(value, ("row", "col"), pairs)


def device(zl, core, x, z, y):
    return (zl * 2 + core) * (NX * NZ * NY) + (x * NZ + z) * NY + y


def shift(value, dx, dy, planes=(0, 1)):
    return permute(
        value, lambda zl, c, x, z, y: (zl, c, (x + dx) % NX, z, (y + dy) % NY) if z in planes else None
    )


def from_first_x(value, dx):
    return permute(value, lambda zl, c, x, z, y: (zl, c, dx, z, y) if x == 0 and z == 0 else None)


def to_second_plane(value):
    return permute(value, lambda zl, c, x, z, y: (zl, c, x, 1, y) if z == 0 else None)


def swap_core(value, planes=(0, 1)):
    return permute(value, lambda zl, c, x, z, y: (zl, 1 - c, x, z, y) if z in planes else None)


def swap_chip(value, j, owners=False):
    return permute(
        value,
        lambda zl, c, x, z, y: (zl ^ j, c, x, z, y) if not owners or (x == 0 and z == 0) else None,
    )


def dot(a, b, dims=NN):
    return lax.dot_general(a, b, dims, preferred_element_type=F32)


def split(value):
    high = value.astype(BF16)
    return high, (value - high.astype(F32)).astype(BF16)


def dot3(a, b):
    ah, al = split(a)
    bh, bl = split(b)
    return dot(jnp.concatenate([ah, ah, al], axis=1), jnp.concatenate([bh, bl, bh], axis=0))


def compact_kernel(place_ref, w_ref, target_ref, out_ref):
    block = place_ref[1]
    rows = lax.broadcasted_iota(jnp.int32, (ACT, BW), 0) + block * ACT
    for group in range(target_ref.shape[0]):
        pick = (rows == target_ref[group, pl.ds(block, 1), :]).astype(F32).astype(BF16)
        slab = w_ref[pl.ds(group * BW * 4, BW, stride=4), :]
        high, rest = split(slab)
        mid, low = split(slab - high.astype(F32))
        out_ref[group] = dot(pick, high, NT) + (dot(pick, mid, NT) + dot(pick, low, NT))


def columns_kernel(place_ref, tri_ref, other_ref, slabs_ref, target_ref, *refs):
    out_refs, full_ref = refs[:NY], refs[NY]
    x, y, zl, core = place_ref[0], place_ref[1], place_ref[2], place_ref[3]
    inner = BW // (2 * NZL)
    for q, half in enumerate((tri_ref, other_ref)):
        for j in range(NZL):
            owner = ((zl ^ j) * 2 + (core ^ q)) * inner
            for b in range(NB):
                full_ref[pl.ds(pl.multiple_of(b * BW + owner, inner), inner), :] = half[
                    (j * NB + b) * inner : (j * NB + b + 1) * inner, :
                ]
    rows = lax.broadcasted_iota(jnp.int32, (ACT, BW), 0) + y * ACT
    tri = full_ref[...]
    high, rest = split(tri)
    mid, low = split(tri - high.astype(F32))
    for s, out_ref in enumerate(out_refs):
        other = (y + s) & (NY - 1)
        pick = (rows == target_ref[other * NX + x, pl.ds(y, 1), :]).astype(F32).astype(BF16)
        out_ref[:, 0 : 4 * BW] = dot(pick, high, NT) + (dot(pick, mid, NT) + dot(pick, low, NT))
        out_ref[:, 4 * BW : 5 * BW] = slabs_ref[other]


def solve_kernel(place_ref, p0, p1, p2, p3, target_ref, out_ref, tri_ref, slab_ref):
    x, y = place_ref[0], place_ref[1]
    group = y * NX + x
    for s, piece in enumerate((p0, p1, p2, p3)):
        block = (y + (NY - s)) & (NY - 1)
        here = pl.ds(pl.multiple_of(block * ACT, ACT), ACT)
        tri_ref[here, :] = piece[:, 0 : 4 * BW]
        slab_ref[here, :] = piece[:, 4 * BW : 5 * BW]
    rows = lax.broadcasted_iota(jnp.int32, (KACT, BW), 0)
    pick = jnp.concatenate(
        [(rows == target_ref[group, b : b + 1, :]).astype(F32).astype(BF16) for b in range(NB)], axis=1
    )
    high, low = split(tri_ref[...])
    active = (dot(high, pick, NT) + dot(low, pick, NT)).T
    row_id = lax.broadcasted_iota(jnp.int32, (KACT, KACT), 0)
    col_ids = lax.broadcasted_iota(jnp.int32, (KACT, KACT), 1)
    diagonal = jnp.where(row_id == col_ids, active, 0.0)
    scale_down = 1.0 / jnp.sum(diagonal, axis=1, keepdims=True)
    scale_across = 1.0 / jnp.sum(diagonal, axis=0, keepdims=True)
    strict = jnp.where(row_id < col_ids, active, 0.0) * scale_down
    differ = row_id ^ col_ids
    inverse = jnp.where(row_id == col_ids, 1.0, 0.0) - jnp.where(differ == 1, strict, 0.0)
    size = 2
    while size < KACT:
        cross = jnp.where((differ >= size) & (differ < 2 * size), strict, 0.0)
        inverse = inverse - dot3(inverse, dot3(cross, inverse))
        size *= 2
    slab = slab_ref[...].T
    out_ref[...] = dot3(slab, inverse) * scale_across


def layout_kernel(place_ref, *refs):
    mine, others = refs[0:2], refs[2:4]
    out_ref = refs[4]
    zl, core = place_ref[2], place_ref[3]
    inner = BW // (2 * NZL)
    for j in range(NZL):
        for q in range(2):
            owner = ((zl ^ j) * 2 + (core ^ q)) * inner
            for b in range(NB):
                for l in range(4):
                    rows = pl.ds(b * inner * 4 + l, inner, stride=4)
                    value = (mine, others)[q][j // 2][j % 2, rows, :]
                    high, low = split(value)
                    for part, piece in enumerate((high, low, high)):
                        start = pl.multiple_of((part * NB + b) * BW + owner, inner)
                        out_ref[pl.ds(start, inner), l * BW : (l + 1) * BW] = piece


def update_kernel(place_ref, w_ref, spread_ref, target_ref, *refs, pieces, first):
    errors = refs[: len(pieces[0])]
    refs = refs[len(pieces[0]) :]
    out_ref, buf_ref, pick_ref, ed_ref, upd_ref, in_sem, out_sem = refs[0 if first else 1 :]
    x, y, owner = place_ref[0], place_ref[1], place_ref[4]
    plan, places = pieces[1], pieces[2]
    which = [((y + (NY - s)) & 3) * NX + ((x + (NX - t)) & 3) for s, t in places]
    size = 4 * BW

    def rows_of(k):
        return pl.ds(pl.multiple_of(which[k] * size, size), size)

    count = len(plan)
    for k in range(count):
        pltpu.make_async_copy(w_ref.at[rows_of(k)], buf_ref.at[k], in_sem.at[k]).start()
    pick_ref[...] = jnp.zeros_like(pick_ref)
    rows = lax.broadcasted_iota(jnp.int32, (ACT, BW), 0)
    start = 0
    while start < count:
        many = min(3, count - start)
        for k in range(start, start + many):
            group = which[k]
            for b in range(NB):
                pick = (rows + b * ACT == target_ref[group, b : b + 1, :]).astype(F32).astype(BF16)
                pick_ref[b * ACT : (b + 1) * ACT, b * BW : (b + 1) * BW] = pick
            pick = pick_ref[...]
            here = slice((k - start) * BW, (k - start + 1) * BW)
            what = plan[k]
            if len(what) == 1:
                value = errors[what[0]][...]
            else:
                (r0, i0), (r1, i1) = what
                value = jnp.concatenate([errors[r0][i0], errors[r1][i1]], axis=0)
            high, low = split(value)
            wide = NB * BW
            high = dot(high, pick).astype(BF16)
            ed_ref[here, 0:wide] = high
            ed_ref[here, wide : 2 * wide] = high
            ed_ref[here, 2 * wide :] = dot(low, pick).astype(BF16)
        span = slice(0, many * BW)
        upd_ref[span, :] = dot(ed_ref[span, :], spread_ref[...])
        for k in range(start, start + many):
            group = which[k]
            pltpu.make_async_copy(w_ref.at[rows_of(k)], buf_ref.at[k], in_sem.at[k]).wait()
            kept = (target_ref[group, pl.ds(y, 1), :] < 0) | (owner == 0)
            for l in range(4):
                here = pl.ds(l, BW, stride=4)
                value = buf_ref[k, here, :] - upd_ref[(k - start) * BW : (k - start + 1) * BW, l * BW : (l + 1) * BW]
                if l == 0:
                    value = jnp.where(kept, value, 0.0)
                buf_ref[k, here, :] = value
            pltpu.make_async_copy(buf_ref.at[k], out_ref.at[rows_of(k)], out_sem.at[k]).start()
        start += many
    for k in range(count):
        pltpu.make_async_copy(buf_ref.at[k], out_ref.at[rows_of(k)], out_sem.at[k]).wait()


def whole(shape):
    return pl.BlockSpec(shape, lambda *_: (0,) * len(shape))


SMEM = pl.BlockSpec(memory_space=pltpu.SMEM)


ANY = pl.BlockSpec(memory_space=pl.ANY)


def scalars(*values):
    return jnp.stack([jnp.asarray(v, jnp.int32) for v in values])


def update(place, flat, spread, target, errors, plan, places, earlier=None):
    count = len(plan)
    first = earlier is None
    operands = [place, flat, spread, target, *errors] + ([] if first else [earlier])
    specs = [SMEM, ANY] + [whole(v.shape) for v in operands[2 : 4 + len(errors)]] + ([] if first else [ANY])
    return pl.pallas_call(
        functools.partial(update_kernel, pieces=(errors, plan, places), first=first),
        out_shape=jax.ShapeDtypeStruct(flat.shape, F32),
        in_specs=specs,
        out_specs=ANY,
        input_output_aliases={} if first else {len(operands) - 1: 0},
        scratch_shapes=[
            pltpu.VMEM((count, 4 * BW, BW), F32),
            pltpu.VMEM((KACT, NB * BW), BF16),
            pltpu.VMEM((3 * BW, 3 * NB * BW), BF16),
            pltpu.VMEM((3 * BW, 4 * BW), F32),
            pltpu.SemaphoreType.DMA((count,)),
            pltpu.SemaphoreType.DMA((count,)),
        ],
        compiler_params=pltpu.CompilerParams(vmem_limit_bytes=50 << 20),
        cost_estimate=pl.CostEstimate(flops=count * 2**28, bytes_accessed=count * 2**19, transcendentals=0),
    )(*operands)


def local(weights, factor, keep_masks):
    me, row = lax.axis_index("col"), lax.axis_index("row")
    x, z, y = me >> 3, (me >> 2) & 1, me & 3
    zl, core = row >> 1, row & 1
    groups = keep_masks.shape[0]
    rows = weights.shape[0]
    flat = weights.reshape(rows * 4, BW)
    barrier = lax.optimization_barrier
    place = scalars(x, y, zl, core, (x == 0) & (z == 0))

    with jax.named_scope("triangle_rows"):
        here = factor.reshape(-1, BW)
        near = swap_chip(here, 1)

    with jax.named_scope("compact"):
        pruned = 1 - keep_masks
        before = jnp.triu(jnp.ones((BW, BW), BF16), 1)
        rank = lax.dot_general(
            pruned.astype(BF16), before, (((2,), (0,)), ((), ())), preferred_element_type=F32
        ).astype(jnp.int32)
        target = jnp.where(pruned == 1, rank + ACT * jnp.arange(NB, dtype=jnp.int32)[None, :, None], -1)
        compact = pl.pallas_call(
            compact_kernel,
            out_shape=jax.ShapeDtypeStruct((groups, ACT, BW), F32),
            in_specs=[SMEM, whole(flat.shape), whole((groups, NB, BW))],
            out_specs=whole((groups, ACT, BW)),
            grid=(1,),
            compiler_params=pltpu.CompilerParams(vmem_limit_bytes=40 << 20),
            cost_estimate=pl.CostEstimate(flops=2**30, bytes_accessed=2**24, transcendentals=0),
        )(place, flat, target)

    with jax.named_scope("triangle_pairs"):
        near, compact = barrier((near, compact))
        chips = [jnp.stack([here, near])]
        pair = chips[0].reshape(2, -1, 4, BW)[:, :, 0, :]
        pair_far = swap_chip(pair, 2, True)

    with jax.named_scope("slab_x"):
        by_owner = compact.reshape(NY, NX, ACT, BW)
        moved = [from_first_x(by_owner[:, dx], dx) for dx in (1, 2, 3)]
        slabs = jnp.where(x == 0, by_owner[:, 0], moved[0] + moved[1] + moved[2])

    with jax.named_scope("triangle_x"):
        tri = jnp.concatenate([pair, pair_far]).reshape(-1, BW)
        tri, chips = barrier((tri, chips))
        moved = [from_first_x(tri, dx) for dx in (1, 2, 3)]

    with jax.named_scope("factor_chips"):
        chips = [chips[0], swap_chip(chips[0], 2)]

    with jax.named_scope("triangle_y"):
        tri = jnp.where(x == 0, tri, moved[0] + moved[1] + moved[2])
        other = swap_core(tri)
        mixed = pl.pallas_call(
            columns_kernel,
            out_shape=[jax.ShapeDtypeStruct((ACT, 5 * BW), F32)] * NY,
            in_specs=[SMEM] + [whole(v.shape) for v in (tri, other, slabs, target)],
            out_specs=[whole((ACT, 5 * BW))] * NY,
            grid=(1,),
            scratch_shapes=[pltpu.VMEM((NB * BW, BW), F32)],
            compiler_params=pltpu.CompilerParams(vmem_limit_bytes=16 << 20),
            cost_estimate=pl.CostEstimate(flops=2**28, bytes_accessed=2**20, transcendentals=0),
        )(place, tri, other, slabs, target)
        mixed = [mixed[0]] + [shift(mixed[s], 0, s) for s in (1, 2, 3)]

    with jax.named_scope("triangle_core"):
        mixed, chips = barrier((mixed, chips))

    with jax.named_scope("factor_core"):
        other_chips = [swap_core(piece) for piece in chips]

    with jax.named_scope("solve"):
        errors = pl.pallas_call(
            solve_kernel,
            out_shape=jax.ShapeDtypeStruct((BW, KACT), F32),
            in_specs=[SMEM] + [whole(v.shape) for v in (*mixed, target)],
            out_specs=whole((BW, KACT)),
            grid=(1,),
            scratch_shapes=[
                pltpu.VMEM((KACT, NB * BW), F32),
                pltpu.VMEM((KACT, BW), F32),
            ],
            compiler_params=pltpu.CompilerParams(vmem_limit_bytes=32 << 20),
            cost_estimate=pl.CostEstimate(flops=2**31, bytes_accessed=2**21, transcendentals=0),
        )(place, *mixed, target)

    with jax.named_scope("errors_plane"):
        errors, other_chips = barrier((errors, other_chips))
        errors = jnp.where(z == 1, to_second_plane(errors), errors)

    with jax.named_scope("errors_near"):
        half = BW // 2
        by_y = [shift(errors, 0, s) for s in (1, 2, 3)]
        by_x = [shift(errors, t, 0) for t in (1, 2, 3)]

    with jax.named_scope("layout"):
        spread = pl.pallas_call(
            layout_kernel,
            out_shape=jax.ShapeDtypeStruct((3 * NB * BW, 4 * BW), BF16),
            in_specs=[SMEM] + [whole((2, 4 * BW // 2, BW))] * 4,
            out_specs=whole((3 * NB * BW, 4 * BW)),
            grid=(1,),
            compiler_params=pltpu.CompilerParams(vmem_limit_bytes=16 << 20),
            cost_estimate=pl.CostEstimate(flops=2**28, bytes_accessed=2**23, transcendentals=0),
        )(place, *chips, *other_chips)

    with jax.named_scope("errors_far"):
        top = jnp.stack([piece[:half] for piece in by_y])
        bottom = jnp.stack([piece[half:] for piece in by_x])
        top_x = [shift(top, t, 0) for t in (1, 2, 3)]
        bottom_y = [shift(bottom, 0, s) for s in (1, 2, 3)]

    with jax.named_scope("update"):
        first = [(0, 0)] + [(s, 0) for s in (1, 2, 3)] + [(0, t) for t in (1, 2, 3)]
        out = update(
            place, flat, spread, target,
            [errors, *by_y, *by_x], [(k,) for k in range(7)], first,
        )
        out, top_x, bottom_y = barrier((out, top_x, bottom_y))
        second = [(s, t) for s in (1, 2, 3) for t in (1, 2, 3)]
        out = update(
            place, flat, spread, target,
            [*top_x, *bottom_y], [((t - 1, s - 1), (3 + s - 1, t - 1)) for s, t in second], second, out,
        )
    return out.reshape(weights.shape)


def solution(mesh):
    placed = (P("row", None, "col"), P(None, "row", None, "col"), P("row", None, None))
    return jax.shard_map(
        local, mesh=mesh, in_specs=placed, out_specs=P("row", None, "col"), check_vma=False
    )
```

```python
import functools

import jax
import jax.numpy as jnp
from jax import lax
from jax.experimental import pallas as pl
from jax.experimental.pallas import tpu as pltpu
from jax.sharding import PartitionSpec as P

NX, NZ, NY, NZL = 4, 2, 4, 4
BW = 128
NB = 4
ACT = 64
KACT = NB * ACT
F32, BF16 = jnp.float32, jnp.bfloat16
NN = (((1,), (0,)), ((), ()))
NT = (((1,), (1,)), ((), ()))


def permute(value, move):
    pairs = []
    for row in range(2 * NZL):
        for x in range(NX):
            for z in range(NZ):
                for y in range(NY):
                    target = move(row >> 1, row & 1, x, z, y)
                    if target is not None:
                        zl, core, tx, tz, ty = target
                        pairs.append((device(row >> 1, row & 1, x, z, y), device(zl, core, tx, tz, ty)))
    return lax.ppermute(value, ("row", "col"), pairs)


def device(zl, core, x, z, y):
    return (zl * 2 + core) * (NX * NZ * NY) + (x * NZ + z) * NY + y


def shift(value, dx, dy, planes=(0, 1)):
    return permute(
        value, lambda zl, c, x, z, y: (zl, c, (x + dx) % NX, z, (y + dy) % NY) if z in planes else None
    )


def from_first_x(value, dx):
    return permute(value, lambda zl, c, x, z, y: (zl, c, dx, z, y) if x == 0 and z == 0 else None)


def to_second_plane(value):
    return permute(value, lambda zl, c, x, z, y: (zl, c, x, 1, y) if z == 0 else None)


def swap_core(value, planes=(0, 1)):
    return permute(value, lambda zl, c, x, z, y: (zl, 1 - c, x, z, y) if z in planes else None)


def swap_chip(value, j, owners=False):
    return permute(
        value,
        lambda zl, c, x, z, y: (zl ^ j, c, x, z, y) if not owners or (x == 0 and z == 0) else None,
    )


def dot(a, b, dims=NN):
    return lax.dot_general(a, b, dims, preferred_element_type=F32)


def split(value):
    high = value.astype(BF16)
    return high, (value - high.astype(F32)).astype(BF16)


def dot3(a, b):
    ah, al = split(a)
    bh, bl = split(b)
    return dot(jnp.concatenate([ah, ah, al], axis=1), jnp.concatenate([bh, bl, bh], axis=0))


def compact_kernel(place_ref, w_ref, target_ref, out_ref):
    block = place_ref[1]
    rows = lax.broadcasted_iota(jnp.int32, (ACT, BW), 0) + block * ACT
    for group in range(target_ref.shape[0]):
        pick = (rows == target_ref[group, pl.ds(block, 1), :]).astype(F32).astype(BF16)
        slab = w_ref[pl.ds(group * BW * 4, BW, stride=4), :]
        high, rest = split(slab)
        mid, low = split(slab - high.astype(F32))
        out_ref[group] = dot(pick, high, NT) + (dot(pick, mid, NT) + dot(pick, low, NT))


def columns_kernel(place_ref, tri_ref, other_ref, slabs_ref, target_ref, *refs):
    out_refs, full_ref = refs[:NY], refs[NY]
    x, y, zl, core = place_ref[0], place_ref[1], place_ref[2], place_ref[3]
    inner = BW // (2 * NZL)
    for q, half in enumerate((tri_ref, other_ref)):
        for j in range(NZL):
            owner = ((zl ^ j) * 2 + (core ^ q)) * inner
            for b in range(NB):
                full_ref[pl.ds(pl.multiple_of(b * BW + owner, inner), inner), :] = half[
                    (j * NB + b) * inner : (j * NB + b + 1) * inner, :
                ]
    rows = lax.broadcasted_iota(jnp.int32, (ACT, BW), 0) + y * ACT
    tri = full_ref[...]
    high, rest = split(tri)
    mid, low = split(tri - high.astype(F32))
    for s, out_ref in enumerate(out_refs):
        other = (y + s) & (NY - 1)
        pick = (rows == target_ref[other * NX + x, pl.ds(y, 1), :]).astype(F32).astype(BF16)
        out_ref[:, 0 : 4 * BW] = dot(pick, high, NT) + (dot(pick, mid, NT) + dot(pick, low, NT))
        out_ref[:, 4 * BW : 5 * BW] = slabs_ref[other]


def solve_kernel(place_ref, p0, p1, p2, p3, target_ref, out_ref, tri_ref, slab_ref):
    x, y = place_ref[0], place_ref[1]
    group = y * NX + x
    for s, piece in enumerate((p0, p1, p2, p3)):
        block = (y + (NY - s)) & (NY - 1)
        here = pl.ds(pl.multiple_of(block * ACT, ACT), ACT)
        tri_ref[here, :] = piece[:, 0 : 4 * BW]
        slab_ref[here, :] = piece[:, 4 * BW : 5 * BW]
    rows = lax.broadcasted_iota(jnp.int32, (KACT, BW), 0)
    pick = jnp.concatenate(
        [(rows == target_ref[group, b : b + 1, :]).astype(F32).astype(BF16) for b in range(NB)], axis=1
    )
    high, low = split(tri_ref[...])
    active = (dot(high, pick, NT) + dot(low, pick, NT)).T
    row_id = lax.broadcasted_iota(jnp.int32, (KACT, KACT), 0)
    col_ids = lax.broadcasted_iota(jnp.int32, (KACT, KACT), 1)
    diagonal = jnp.where(row_id == col_ids, active, 0.0)
    scale_down = 1.0 / jnp.sum(diagonal, axis=1, keepdims=True)
    scale_across = 1.0 / jnp.sum(diagonal, axis=0, keepdims=True)
    strict = jnp.where(row_id < col_ids, active, 0.0) * scale_down
    differ = row_id ^ col_ids
    inverse = jnp.where(row_id == col_ids, 1.0, 0.0) - jnp.where(differ == 1, strict, 0.0)
    size = 2
    while size < KACT:
        cross = jnp.where((differ >= size) & (differ < 2 * size), strict, 0.0)
        inverse = inverse - dot3(inverse, dot3(cross, inverse))
        size *= 2
    slab = slab_ref[...].T
    out_ref[...] = dot3(slab, inverse) * scale_across


def layout_kernel(place_ref, *refs):
    mine, others = refs[0:2], refs[2:4]
    out_ref = refs[4]
    zl, core = place_ref[2], place_ref[3]
    inner = BW // (2 * NZL)
    for j in range(NZL):
        for q in range(2):
            owner = ((zl ^ j) * 2 + (core ^ q)) * inner
            for b in range(NB):
                for l in range(4):
                    rows = pl.ds(b * inner * 4 + l, inner, stride=4)
                    value = (mine, others)[q][j // 2][j % 2, rows, :]
                    high, low = split(value)
                    for part, piece in enumerate((high, low, high)):
                        start = pl.multiple_of((part * NB + b) * BW + owner, inner)
                        out_ref[pl.ds(start, inner), l * BW : (l + 1) * BW] = piece


def update_kernel(place_ref, w_ref, spread_ref, target_ref, *refs, pieces, first):
    errors = refs[: len(pieces[0])]
    refs = refs[len(pieces[0]) :]
    out_ref, buf_ref, pick_ref, ed_ref, upd_ref, in_sem, out_sem = refs[0 if first else 1 :]
    x, y, owner = place_ref[0], place_ref[1], place_ref[4]
    plan, places = pieces[1], pieces[2]
    which = [((y + (NY - s)) & 3) * NX + ((x + (NX - t)) & 3) for s, t in places]
    size = 4 * BW

    def rows_of(k):
        return pl.ds(pl.multiple_of(which[k] * size, size), size)

    count = len(plan)
    for k in range(count):
        pltpu.make_async_copy(w_ref.at[rows_of(k)], buf_ref.at[k], in_sem.at[k]).start()
    pick_ref[...] = jnp.zeros_like(pick_ref)
    rows = lax.broadcasted_iota(jnp.int32, (ACT, BW), 0)
    start = 0
    while start < count:
        many = min(3, count - start)
        for k in range(start, start + many):
            group = which[k]
            for b in range(NB):
                pick = (rows + b * ACT == target_ref[group, b : b + 1, :]).astype(F32).astype(BF16)
                pick_ref[b * ACT : (b + 1) * ACT, b * BW : (b + 1) * BW] = pick
            pick = pick_ref[...]
            here = slice((k - start) * BW, (k - start + 1) * BW)
            what = plan[k]
            parts = [errors[ref][begin:end, :] for ref, begin, end in what]
            value = parts[0] if len(parts) == 1 else jnp.concatenate(parts, axis=0)
            high, low = split(value)
            wide = NB * BW
            high = dot(high, pick).astype(BF16)
            ed_ref[here, 0:wide] = high
            ed_ref[here, wide : 2 * wide] = high
            ed_ref[here, 2 * wide :] = dot(low, pick).astype(BF16)
        span = slice(0, many * BW)
        upd_ref[span, :] = dot(ed_ref[span, :], spread_ref[...])
        for k in range(start, start + many):
            group = which[k]
            pltpu.make_async_copy(w_ref.at[rows_of(k)], buf_ref.at[k], in_sem.at[k]).wait()
            kept = (target_ref[group, pl.ds(y, 1), :] < 0) | (owner == 0)
            for l in range(4):
                here = pl.ds(l, BW, stride=4)
                value = buf_ref[k, here, :] - upd_ref[(k - start) * BW : (k - start + 1) * BW, l * BW : (l + 1) * BW]
                if l == 0:
                    value = jnp.where(kept, value, 0.0)
                buf_ref[k, here, :] = value
            pltpu.make_async_copy(buf_ref.at[k], out_ref.at[rows_of(k)], out_sem.at[k]).start()
        start += many
    for k in range(count):
        pltpu.make_async_copy(buf_ref.at[k], out_ref.at[rows_of(k)], out_sem.at[k]).wait()


def whole(shape):
    return pl.BlockSpec(shape, lambda *_: (0,) * len(shape))


SMEM = pl.BlockSpec(memory_space=pltpu.SMEM)


ANY = pl.BlockSpec(memory_space=pl.ANY)


def scalars(*values):
    return jnp.stack([jnp.asarray(v, jnp.int32) for v in values])


def update(place, flat, spread, target, errors, plan, places, earlier=None):
    count = len(plan)
    first = earlier is None
    operands = [place, flat, spread, target, *errors] + ([] if first else [earlier])
    specs = [SMEM, ANY] + [whole(v.shape) for v in operands[2 : 4 + len(errors)]] + ([] if first else [ANY])
    return pl.pallas_call(
        functools.partial(update_kernel, pieces=(errors, plan, places), first=first),
        out_shape=jax.ShapeDtypeStruct(flat.shape, F32),
        in_specs=specs,
        out_specs=ANY,
        input_output_aliases={} if first else {len(operands) - 1: 0},
        scratch_shapes=[
            pltpu.VMEM((count, 4 * BW, BW), F32),
            pltpu.VMEM((KACT, NB * BW), BF16),
            pltpu.VMEM((3 * BW, 3 * NB * BW), BF16),
            pltpu.VMEM((3 * BW, 4 * BW), F32),
            pltpu.SemaphoreType.DMA((count,)),
            pltpu.SemaphoreType.DMA((count,)),
        ],
        compiler_params=pltpu.CompilerParams(vmem_limit_bytes=50 << 20),
        cost_estimate=pl.CostEstimate(flops=count * 2**28, bytes_accessed=count * 2**19, transcendentals=0),
    )(*operands)


def far_parts(s, t):
    half = BW // 2
    if s == 2 and t == 2:
        return [(1, 0, half), (4, 0, half)]
    if s == 2:
        return [(t - 1, BW, 2 * BW)]
    if t == 2:
        return [(2 + s, BW, 2 * BW)]
    return [(t - 1, (s // 2) * half, (s // 2 + 1) * half), (2 + s, (t // 2) * half, (t // 2 + 1) * half)]


def local(weights, factor, keep_masks):
    me, row = lax.axis_index("col"), lax.axis_index("row")
    x, z, y = me >> 3, (me >> 2) & 1, me & 3
    zl, core = row >> 1, row & 1
    groups = keep_masks.shape[0]
    rows = weights.shape[0]
    flat = weights.reshape(rows * 4, BW)
    barrier = lax.optimization_barrier
    place = scalars(x, y, zl, core, (x == 0) & (z == 0))

    with jax.named_scope("triangle_rows"):
        here = factor.reshape(-1, BW)
        near = swap_chip(here, 1)

    with jax.named_scope("compact"):
        pruned = 1 - keep_masks
        before = jnp.triu(jnp.ones((BW, BW), BF16), 1)
        rank = lax.dot_general(
            pruned.astype(BF16), before, (((2,), (0,)), ((), ())), preferred_element_type=F32
        ).astype(jnp.int32)
        target = jnp.where(pruned == 1, rank + ACT * jnp.arange(NB, dtype=jnp.int32)[None, :, None], -1)
        compact = pl.pallas_call(
            compact_kernel,
            out_shape=jax.ShapeDtypeStruct((groups, ACT, BW), F32),
            in_specs=[SMEM, whole(flat.shape), whole((groups, NB, BW))],
            out_specs=whole((groups, ACT, BW)),
            grid=(1,),
            compiler_params=pltpu.CompilerParams(vmem_limit_bytes=40 << 20),
            cost_estimate=pl.CostEstimate(flops=2**30, bytes_accessed=2**24, transcendentals=0),
        )(place, flat, target)

    with jax.named_scope("triangle_pairs"):
        near, compact = barrier((near, compact))
        chips = [jnp.stack([here, near])]
        pair = chips[0].reshape(2, -1, 4, BW)[:, :, 0, :]
        pair_far = swap_chip(pair, 2, True)

    with jax.named_scope("slab_x"):
        by_owner = compact.reshape(NY, NX, ACT, BW)
        moved = [from_first_x(by_owner[:, dx], dx) for dx in (1, 2, 3)]
        slabs = jnp.where(x == 0, by_owner[:, 0], moved[0] + moved[1] + moved[2])

    with jax.named_scope("triangle_x"):
        tri = jnp.concatenate([pair, pair_far]).reshape(-1, BW)
        tri, chips = barrier((tri, chips))
        moved = [from_first_x(tri, dx) for dx in (1, 2, 3)]

    with jax.named_scope("factor_chips"):
        chips = [chips[0], swap_chip(chips[0], 2)]

    with jax.named_scope("triangle_y"):
        tri = jnp.where(x == 0, tri, moved[0] + moved[1] + moved[2])
        other = swap_core(tri)
        mixed = pl.pallas_call(
            columns_kernel,
            out_shape=[jax.ShapeDtypeStruct((ACT, 5 * BW), F32)] * NY,
            in_specs=[SMEM] + [whole(v.shape) for v in (tri, other, slabs, target)],
            out_specs=[whole((ACT, 5 * BW))] * NY,
            grid=(1,),
            scratch_shapes=[pltpu.VMEM((NB * BW, BW), F32)],
            compiler_params=pltpu.CompilerParams(vmem_limit_bytes=16 << 20),
            cost_estimate=pl.CostEstimate(flops=2**28, bytes_accessed=2**20, transcendentals=0),
        )(place, tri, other, slabs, target)
        mixed = [mixed[0]] + [shift(mixed[s], 0, s) for s in (1, 2, 3)]

    with jax.named_scope("triangle_core"):
        mixed, chips = barrier((mixed, chips))

    with jax.named_scope("factor_core"):
        other_chips = [swap_core(piece) for piece in chips]

    with jax.named_scope("solve"):
        errors = pl.pallas_call(
            solve_kernel,
            out_shape=jax.ShapeDtypeStruct((BW, KACT), F32),
            in_specs=[SMEM] + [whole(v.shape) for v in (*mixed, target)],
            out_specs=whole((BW, KACT)),
            grid=(1,),
            scratch_shapes=[
                pltpu.VMEM((KACT, NB * BW), F32),
                pltpu.VMEM((KACT, BW), F32),
            ],
            compiler_params=pltpu.CompilerParams(vmem_limit_bytes=32 << 20),
            cost_estimate=pl.CostEstimate(flops=2**31, bytes_accessed=2**21, transcendentals=0),
        )(place, *mixed, target)

    with jax.named_scope("errors_plane"):
        errors, other_chips = barrier((errors, other_chips))
        errors = jnp.where(z == 1, to_second_plane(errors), errors)

    with jax.named_scope("errors_near"):
        half = BW // 2
        by_y = [shift(errors, 0, s) for s in (1, 2, 3)]
        by_x = [shift(errors, t, 0) for t in (1, 2, 3)]

    with jax.named_scope("layout"):
        spread = pl.pallas_call(
            layout_kernel,
            out_shape=jax.ShapeDtypeStruct((3 * NB * BW, 4 * BW), BF16),
            in_specs=[SMEM] + [whole((2, 4 * BW // 2, BW))] * 4,
            out_specs=whole((3 * NB * BW, 4 * BW)),
            grid=(1,),
            compiler_params=pltpu.CompilerParams(vmem_limit_bytes=16 << 20),
            cost_estimate=pl.CostEstimate(flops=2**28, bytes_accessed=2**23, transcendentals=0),
        )(place, *chips, *other_chips)

    with jax.named_scope("errors_far"):
        top = jnp.concatenate([by_y[0][:half], by_y[2][:half], by_y[1]])
        bottom = jnp.concatenate([by_x[0][half:], by_x[2][half:], by_x[1]])
        top_x = [shift(top, 1, 0), shift(by_y[1][:half], 2, 0), shift(top, 3, 0)]
        bottom_y = [shift(bottom, 0, 1), shift(by_x[1][half:], 0, 2), shift(bottom, 0, 3)]

    with jax.named_scope("update"):
        first = [(0, 0)] + [(s, 0) for s in (1, 2, 3)] + [(0, t) for t in (1, 2, 3)]
        out = update(
            place, flat, spread, target,
            [errors, *by_y, *by_x], [[(k, 0, BW)] for k in range(7)], first,
        )
        out, top_x, bottom_y = barrier((out, top_x, bottom_y))
        second = [(s, t) for s in (1, 2, 3) for t in (1, 2, 3)]
        out = update(
            place, flat, spread, target,
            [*top_x, *bottom_y], [far_parts(s, t) for s, t in second], second, out,
        )
    return out.reshape(weights.shape)


def solution(mesh):
    placed = (P("row", None, "col"), P(None, "row", None, "col"), P("row", None, None))
    return jax.shard_map(
        local, mesh=mesh, in_specs=placed, out_specs=P("row", None, "col"), check_vma=False
    )
```
